256 devices in a mesh: rollout: 8 (over y, z_lo), shard: 32 (over z_hi, x, core).
Axes of the slice: x: 4, y: 4, z: 8 (z_hi: 4, z_lo: 2; z = z_hi * 2 + z_lo), core: 2. Of those that a mesh axis runs over, the one named last changes fastest.
Arguments:
- updated: bfloat16 [12, 7168, 1024], P(None, 'shard', 'rollout'), may hold values from -6 to 6
- trainer_base: bfloat16 [12, 7168, 1024], P(None, 'shard', 'rollout'), may hold values from -6 to 6
- rollout_base: bfloat16 [32, 1792, 1024], P('shard'), may hold values from -6 to 6
- sync_ids: int32 [8], replicated, may hold values from 0 to 11, as said below
- owner_map: int32 [8], replicated, may hold values from 0 to 7, each once
Outputs:
- synced: bfloat16 [32, 1792, 1024], P('shard')
The draws below stay inside these ranges and needn't reach their ends.
Inputs may be any that keep to these rules, and one draw needn't show every extreme that they name: `sync_ids`: the ids are distinct. `owner_map`: each position appears once.
All inputs are finite; a program needn't handle non-finite values.
Results may differ from the reference program's by a relative error of at most 0.001.
Values may be sent and summed in bfloat16 or wider, within the bound.
No kernel may reach another device: no remote copies, remote signals or barrier semaphores. Data moves between devices by JAX's collectives and lax.ppermute only.
A program may use at most 128 MiB of HBM per device.

```python
import jax
import jax.numpy as jnp
from jax import lax

D = 7168
FF = 1024
BLOCK = 128
EXPERTS = 8
TRAIN_EXP = 12
OWN_SPLIT = 4
PIECE = 56
ROWS_OWN = 1792
N_SHARD = 32


def draw_sync_ids(key, part):
    key = jax.random.fold_in(key, 7)
    middle = jax.random.permutation(key, TRAIN_EXP - 2).astype(jnp.int32) + 1
    ends = jnp.array([0, TRAIN_EXP - 1], jnp.int32)
    chosen = jnp.concatenate([ends, middle[:EXPERTS - 2]])
    return jax.random.permutation(jax.random.fold_in(key, 1), chosen).astype(jnp.int32)


def block_levels(own_key, shape, cuts, least, top_value):
    def one(position, shards_of):
        steps = jax.random.uniform(jax.random.fold_in(jax.random.fold_in(own_key, 6), position), (shards_of,), jnp.float32, least / len(cuts), top_value / len(cuts))
        return jnp.repeat(jnp.exp(steps), shape[position] // shards_of).reshape((-1,) + (1,) * (len(shape) - position - 1))

    factor_of = one(*cuts[0])
    for cut in cuts[1:]:
        factor_of = factor_of * one(*cut)
    return factor_of


def noise(stream_key, extent, spread, bound, pieces=(), held_as=jnp.bfloat16):
    entries = jax.random.normal(stream_key, extent, jnp.float32) * spread
    if len(pieces) > 0:
        entries = block_levels(stream_key, extent, pieces, -0.22, 0.18) * entries
    return jnp.clip(entries, min=-bound, max=bound).astype(held_as)


def setup_inputs(seed: int = 0) -> dict:
    keys = jax.random.split(jax.random.key(seed), 6)
    updated = noise(keys[0], (TRAIN_EXP, D, FF), 1.0, 6.0, ((1, 32), (2, 8)))
    trainer_base = noise(keys[1], (TRAIN_EXP, D, FF), 1.0, 6.0, ((1, 32), (2, 8)))
    rollout_base = noise(keys[2], (EXPERTS * OWN_SPLIT, ROWS_OWN, FF), 1.0, 6.0, ((0, 32),))
    sync_ids = draw_sync_ids(jax.random.fold_in(keys[5], 71), 0)
    owner_map = jax.random.permutation(keys[4], EXPERTS).astype(jnp.int32)
    return {"updated": updated, "trainer_base": trainer_base, "rollout_base": rollout_base, "sync_ids": sync_ids, "owner_map": owner_map}


def block_scale(largest):
    scale = jnp.full_like(largest, 2.0 ** -24)
    for power in range(-24, 8):
        scale = jnp.where(largest > 448.0 * 2.0 ** power, scale * 2.0, scale)
    return scale


def onto_grid(ratio):
    magnitude = jnp.abs(ratio)
    spacing = jnp.full_like(magnitude, 2.0 ** -9)
    for power in range(-5, 9):
        spacing = jnp.where(magnitude >= 2.0 ** power, spacing * 2.0, spacing)
    return jnp.sign(ratio) * spacing * jnp.floor(magnitude / spacing + 0.5)


def reference(updated, trainer_base, rollout_base, sync_ids, owner_map):
    fresh = jnp.take(updated, sync_ids.astype(jnp.int32), axis=0).astype(jnp.float32)
    older = jnp.take(trainer_base, sync_ids.astype(jnp.int32), axis=0).astype(jnp.float32)
    delta = fresh - older
    blocks = delta.reshape(EXPERTS, D, FF // BLOCK, BLOCK)
    largest = jnp.max(jnp.abs(blocks), axis=3, keepdims=True)
    scale = block_scale(largest).astype(jnp.bfloat16)
    scale = lax.optimization_barrier(scale).astype(jnp.float32)
    code = onto_grid(blocks / scale).astype(jnp.bfloat16)
    code = lax.optimization_barrier(code).astype(jnp.float32)
    value = (code * scale).reshape(EXPERTS, D, FF)
    inverse = jnp.argsort(owner_map).astype(jnp.int32)
    value = jnp.take(value, inverse, axis=0)
    value = value.reshape(EXPERTS, N_SHARD, OWN_SPLIT, PIECE, FF)
    value = jnp.transpose(value, (0, 2, 1, 3, 4)).reshape(EXPERTS * OWN_SPLIT, N_SHARD * PIECE, FF)
    return (rollout_base.astype(jnp.float32) + value).astype(jnp.bfloat16)
```

```python
import jax
import jax.numpy as jnp
from jax import lax
from jax.experimental import pallas as pl
from jax.experimental.pallas import tpu as pltpu
from jax.sharding import PartitionSpec as P

EXPERTS = 8
ROWS = 224
BLOCK = 128
PIECE = 56
OWNED = 1792
WIDTH = 1024
HALF = OWNED // 2
CHUNK = 448


def floor_power(magnitude):
    spread = magnitude * (2.0**23 + 1.0)
    power = spread - (spread - magnitude)
    return jnp.where(power > magnitude, power * 0.5, power)


def quantize(fresh, older):
    delta = fresh.astype(jnp.float32) - older.astype(jnp.float32)
    magnitude = jnp.abs(delta)
    largest = jnp.max(magnitude, axis=-1, keepdims=True)
    power = floor_power(largest)
    scale = jnp.where(largest > 1.75 * power, power * 2.0**-7, power * 2.0**-8)
    scale = jnp.maximum(scale, 2.0**-24)
    binade = jnp.maximum(floor_power(magnitude), scale * 2.0**-6)
    shift = binade * (1.5 * 2.0**20)
    rounded = (magnitude + shift) - shift
    tie = (magnitude - rounded) >= binade * 2.0**-4
    rounded = jnp.where(tie, rounded + binade * 2.0**-3, rounded)
    return jnp.where(delta < 0.0, -rounded, rounded).astype(jnp.bfloat16)


def encode_kernel(ids_ref, owner_ref, fresh_ref, older_ref, value_ref):
    value_ref[...] = quantize(fresh_ref[...], older_ref[...])


def encode(updated, trainer_base, sync_ids, owner_map):
    picked = pl.BlockSpec((1, ROWS, BLOCK), lambda e, ids, owner: (ids[e], 0, 0))
    placed = pl.BlockSpec((1, ROWS, BLOCK), lambda e, ids, owner: (owner[e], 0, 0))
    return pl.pallas_call(
        encode_kernel,
        grid_spec=pltpu.PrefetchScalarGridSpec(
            num_scalar_prefetch=2,
            grid=(EXPERTS,),
            in_specs=[picked, picked],
            out_specs=placed,
        ),
        out_shape=jax.ShapeDtypeStruct((EXPERTS, ROWS, BLOCK), jnp.bfloat16),
        name="encode",
    )(sync_ids, owner_map, updated, trainer_base)


def shifted(block, dy=0, dz=0):
    pairs = []
    for y in range(4):
        for z in range(2):
            pairs.append((y * 2 + z, (y + dy) % 4 * 2 + (z + dz) % 2))
    return lax.ppermute(block, "rollout", pairs)


def add_kernel(where_ref, base_ref, *refs):
    blocks, out_ref = refs[:-1], refs[-1]
    first = pl.program_id(0) < 2

    def put(k, value):
        columns = pl.ds(pl.multiple_of(where_ref[k] * BLOCK, BLOCK), BLOCK)
        total = base_ref[:, columns].astype(jnp.float32) + value.astype(jnp.float32)
        out_ref[:, columns] = total.astype(jnp.bfloat16)

    for k in range(6):
        put(k, blocks[k][...])
    for k in (6, 7):
        a, b = blocks[2 * k - 6], blocks[2 * k - 5]

        @pl.when(first)
        def _():
            put(k, a[...])

        @pl.when(jnp.logical_not(first))
        def _():
            put(k, b[...])


def add(where, base, whole, halves):
    row = pl.BlockSpec((CHUNK, WIDTH), lambda i, w: (i, 0))
    full = pl.BlockSpec((CHUNK, BLOCK), lambda i, w: (i, 0))
    upper = pl.BlockSpec((CHUNK, BLOCK), lambda i, w: (jnp.minimum(i, 1), 0))
    lower = pl.BlockSpec((CHUNK, BLOCK), lambda i, w: (jnp.maximum(i - 2, 0), 0))
    return pl.pallas_call(
        add_kernel,
        grid_spec=pltpu.PrefetchScalarGridSpec(
            num_scalar_prefetch=1,
            grid=(OWNED // CHUNK,),
            in_specs=[row] + [full] * 6 + [upper, lower] * 2,
            out_specs=row,
        ),
        out_shape=jax.ShapeDtypeStruct((OWNED, WIDTH), jnp.bfloat16),
        compiler_params=pltpu.CompilerParams(vmem_limit_bytes=32 * 2**20),
        name="add",
    )(where, base, *whole, *halves)


def per_device(updated, trainer_base, rollout_base, sync_ids, owner_map):
    values = encode(updated, trainer_base, sync_ids, owner_map)
    values = values.reshape(32, PIECE, BLOCK)
    own = lax.all_to_all(values, "shard", split_axis=0, concat_axis=0, tiled=True)
    own = own.reshape(OWNED, BLOCK)
    below, above, beside = shifted(own, dy=1), shifted(own, dy=-1), shifted(own, dz=1)
    far_a, far_b = shifted(below[:HALF], dy=1), shifted(above[HALF:], dy=-1)
    beside_below, beside_above = shifted(beside, dy=1), shifted(beside, dy=-1)
    beside_a, beside_b = shifted(far_a, dz=1), shifted(far_b, dz=1)
    me = lax.axis_index("rollout")
    y, z = me // 2, me % 2
    at = lambda dy, dz: (y + dy) % 4 * 2 + (z + dz) % 2
    where = jnp.stack(
        [at(0, 0), at(-1, 0), at(1, 0), at(0, 1), at(-1, 1), at(1, 1), at(2, 0), at(2, 1)]
    ).astype(jnp.int32)
    whole = [own, below, above, beside, beside_below, beside_above]
    halves = [far_a, far_b, beside_a, beside_b]
    return add(where, rollout_base[0], whole, halves)[None]


def solution(mesh):
    return jax.shard_map(
        per_device,
        mesh=mesh,
        in_specs=(
            P(None, "shard", "rollout"),
            P(None, "shard", "rollout"),
            P("shard", None, None),
            P(),
            P(),
        ),
        out_specs=P("shard", None, None),
        check_vma=False,
    )
```

```python
import jax
import jax.numpy as jnp
from jax import lax
from jax.experimental import pallas as pl
from jax.experimental.pallas import tpu as pltpu
from jax.sharding import PartitionSpec as P

EXPERTS = 8
ROWS = 224
BLOCK = 128
PIECE = 56
OWNED = 1792
WIDTH = 1024
CHUNK = 448
HALF = OWNED // 2
FIRST = 4


def floor_power(magnitude):
    spread = magnitude * (2.0**23 + 1.0)
    power = spread - (spread - magnitude)
    return jnp.where(power > magnitude, power * 0.5, power)


def quantize(fresh, older):
    delta = fresh.astype(jnp.float32) - older.astype(jnp.float32)
    magnitude = jnp.abs(delta)
    largest = jnp.max(magnitude, axis=-1, keepdims=True)
    power = floor_power(largest)
    scale = jnp.where(largest > 1.75 * power, power * 2.0**-7, power * 2.0**-8)
    scale = jnp.maximum(scale, 2.0**-24)
    binade = jnp.maximum(floor_power(magnitude), scale * 2.0**-6)
    shift = binade * (1.5 * 2.0**20)
    rounded = (magnitude + shift) - shift
    tie = (magnitude - rounded) >= binade * 2.0**-4
    rounded = jnp.where(tie, rounded + binade * 2.0**-3, rounded)
    return jnp.where(delta < 0.0, -rounded, rounded)


def encode_kernel(ids_ref, owner_ref, fresh_hbm, older_hbm, value_ref, fresh_ref, older_ref, sems):
    def copies(e):
        slot = ids_ref[e]
        return (
            pltpu.make_async_copy(fresh_hbm.at[slot], fresh_ref.at[e], sems.at[0, e]),
            pltpu.make_async_copy(older_hbm.at[slot], older_ref.at[e], sems.at[1, e]),
        )

    for e in range(EXPERTS):
        for copy in copies(e):
            copy.start()

    @pl.loop(0, EXPERTS)
    def _(e):
        for copy in copies(e):
            copy.wait()
        value_ref[owner_ref[e]] = quantize(fresh_ref[e], older_ref[e]).astype(jnp.bfloat16)


def encode(updated, trainer_base, sync_ids, owner_map):
    return pl.pallas_call(
        encode_kernel,
        in_specs=[pl.BlockSpec(memory_space=pltpu.SMEM)] * 2 + [pl.BlockSpec(memory_space=pl.ANY)] * 2,
        out_specs=pl.BlockSpec(memory_space=pltpu.VMEM),
        out_shape=jax.ShapeDtypeStruct((EXPERTS, ROWS, BLOCK), jnp.bfloat16),
        scratch_shapes=[
            pltpu.VMEM((EXPERTS, ROWS, BLOCK), jnp.bfloat16),
            pltpu.VMEM((EXPERTS, ROWS, BLOCK), jnp.bfloat16),
            pltpu.SemaphoreType.DMA((2, EXPERTS)),
        ],
        name="encode",
    )(sync_ids, owner_map, updated, trainer_base)


def shifted(block, dy=0, dz=0):
    pairs = []
    for y in range(4):
        for z in range(2):
            pairs.append((y * 2 + z, (y + dy) % 4 * 2 + (z + dz) % 2))
    return lax.ppermute(block, "rollout", pairs)


def add_kernel(where_ref, base_ref, *refs):
    out_ref, rest_ref = refs[-2:]
    step = pl.program_id(0)
    rows = pl.ds(pl.multiple_of(step % 2 * CHUNK, CHUNK), CHUNK)

    def columns(k):
        return pl.ds(pl.multiple_of(where_ref[k] * BLOCK, BLOCK), BLOCK)

    for k in range(FIRST, 8):
        rest_ref[k - FIRST] = base_ref[:, columns(k)]
    for half in range(2):

        @pl.when(step // 2 == half)
        def _():
            for k in range(FIRST):
                out_ref[:, columns(k)] = base_ref[:, columns(k)] + refs[2 * k + half][rows, :]


def add(where, base, parts):
    band = pl.BlockSpec((CHUNK, WIDTH), lambda i, w: (i, 0))
    return pl.pallas_call(
        add_kernel,
        grid_spec=pltpu.PrefetchScalarGridSpec(
            num_scalar_prefetch=1,
            grid=(OWNED // CHUNK,),
            in_specs=[band] + [pl.BlockSpec(memory_space=pltpu.VMEM)] * len(parts),
            out_specs=[band, pl.BlockSpec((8 - FIRST, CHUNK, BLOCK), lambda i, w: (0, i, 0))],
        ),
        out_shape=[
            jax.ShapeDtypeStruct((OWNED, WIDTH), jnp.bfloat16),
            jax.ShapeDtypeStruct((8 - FIRST, OWNED, BLOCK), jnp.bfloat16),
        ],
        compiler_params=pltpu.CompilerParams(vmem_limit_bytes=12 * 2**20),
        cost_estimate=pl.CostEstimate(flops=OWNED * WIDTH, bytes_accessed=6 * OWNED * WIDTH, transcendentals=0),
        name="add",
    )(where, base, *parts)


def finish_kernel(where_ref, rest_ref, *refs):
    parts, (out_hbm, total_ref, sems) = refs[:-4], refs[-3:]
    copies = []
    for k in range(FIRST, 8):
        column = pl.ds(pl.multiple_of(where_ref[k] * BLOCK, BLOCK), BLOCK)
        n = k - FIRST
        for half in range(2):
            rows = pl.ds(half * HALF, HALF)
            total_ref[n, rows, :] = rest_ref[n, rows, :] + parts[2 * n + half][...]
            copies.append(pltpu.make_async_copy(total_ref.at[n, rows], out_hbm.at[rows, column], sems.at[n, half]))
            copies[-1].start()
    for copy in copies:
        copy.wait()


def finish(where, rest, parts, made):
    whole = pl.BlockSpec(memory_space=pltpu.VMEM)
    return pl.pallas_call(
        finish_kernel,
        in_specs=[pl.BlockSpec(memory_space=pltpu.SMEM), whole] + [whole] * len(parts) + [pl.BlockSpec(memory_space=pl.ANY)],
        out_specs=pl.BlockSpec(memory_space=pl.ANY),
        out_shape=jax.ShapeDtypeStruct((OWNED, WIDTH), jnp.bfloat16),
        scratch_shapes=[pltpu.VMEM((8 - FIRST, OWNED, BLOCK), jnp.bfloat16), pltpu.SemaphoreType.DMA((8 - FIRST, 2))],
        input_output_aliases={2 + len(parts): 0},
        compiler_params=pltpu.CompilerParams(vmem_limit_bytes=8 * 2**20),
        name="finish",
    )(where, rest, *parts, made)


def gather(own):
    own_a, own_b = own[:HALF], own[HALF:]
    beside_a, beside_b = shifted(own_a, dz=1), shifted(own_b, dz=1)
    below_a, above_b = shifted(own_a, dy=1), shifted(own_b, dy=-1)
    below_b, above_a = shifted(own_b, dy=1), shifted(own_a, dy=-1)
    bb_a, ba_b = shifted(beside_a, dy=1), shifted(beside_b, dy=-1)
    far_a, far_b = shifted(below_a, dy=1), shifted(above_b, dy=-1)
    bb_b, ba_a = shifted(below_b, dz=1), shifted(above_a, dz=1)
    fz_a, fz_b = shifted(bb_a, dy=1), shifted(ba_b, dy=-1)
    early = [own_a, own_b, below_a, below_b, above_a, above_b, beside_a, beside_b]
    return early, [far_a, far_b, bb_a, bb_b, ba_a, ba_b, fz_a, fz_b]


def per_device(updated, trainer_base, rollout_base, sync_ids, owner_map):
    values = encode(updated, trainer_base, sync_ids, owner_map).reshape(32, PIECE, BLOCK)
    own = lax.all_to_all(values, "shard", split_axis=0, concat_axis=0, tiled=True)
    early, late = gather(own.reshape(OWNED, BLOCK))
    me = lax.axis_index("rollout")
    y, z = me // 2, me % 2
    moves = [(0, 0), (-1, 0), (1, 0), (0, 1), (2, 0), (-1, 1), (1, 1), (2, 1)]
    where = jnp.stack([(y + dy) % 4 * 2 + (z + dz) % 2 for dy, dz in moves]).astype(jnp.int32)
    made, rest = add(where, rollout_base[0], early)
    return finish(where, rest, late, made)[None]


def solution(mesh):
    return jax.shard_map(
        per_device,
        mesh=mesh,
        in_specs=(
            P(None, "shard", "rollout"),
            P(None, "shard", "rollout"),
            P("shard", None, None),
            P(),
            P(),
        ),
        out_specs=P("shard", None, None),
        check_vma=False,
    )
```

```python
import functools

import jax
import jax.numpy as jnp
from jax import lax
from jax.experimental import pallas as pl
from jax.experimental.pallas import tpu as pltpu
from jax.sharding import PartitionSpec as P

EXPERTS = 8
ROWS = 224
BLOCK = 128
PIECE = 56
OWNED = 1792
WIDTH = 1024
BAND = 448
SPLIT = 896
FIRST = 4
MOVES = [(0, 0), (-1, 0), (1, 0), (0, 1), (2, 0), (-1, 1), (1, 1), (2, 1)]


def floor_power(magnitude):
    spread = magnitude * (2.0**23 + 1.0)
    power = spread - (spread - magnitude)
    return jnp.where(power > magnitude, power * 0.5, power)


def quantize(fresh, older):
    delta = fresh.astype(jnp.float32) - older.astype(jnp.float32)
    magnitude = jnp.abs(delta)
    largest = jnp.max(magnitude, axis=-1, keepdims=True)
    power = floor_power(largest)
    scale = jnp.where(largest > 1.75 * power, power * 2.0**-7, power * 2.0**-8)
    scale = jnp.maximum(scale, 2.0**-24)
    binade = jnp.maximum(floor_power(magnitude), scale * 2.0**-6)
    shift = binade * (1.5 * 2.0**20)
    rounded = (magnitude + shift) - shift
    tie = (magnitude - rounded) >= binade * 2.0**-4
    rounded = jnp.where(tie, rounded + binade * 2.0**-3, rounded)
    return jnp.where(delta < 0.0, -rounded, rounded)


def encode_kernel(ids_hbm, owner_hbm, fresh_hbm, older_hbm, value_ref, ids_ref, owner_ref, fresh_ref, older_ref, sems, few):
    ids = pltpu.make_async_copy(ids_hbm, ids_ref, few.at[0])
    owner = pltpu.make_async_copy(owner_hbm, owner_ref, few.at[1])
    ids.start()
    owner.start()
    slots = fresh_ref.shape[0]
    copies = []
    for slot in range(slots):
        fresh = pltpu.make_async_copy(fresh_hbm.at[slot], fresh_ref.at[slot], sems.at[0, slot])
        older = pltpu.make_async_copy(older_hbm.at[slot], older_ref.at[slot], sems.at[1, slot])
        fresh.start()
        older.start()
        copies += [fresh, older]
    ids.wait()
    owner.wait()
    for copy in copies:
        copy.wait()

    @pl.loop(0, EXPERTS)
    def _(e):
        slot = ids_ref[e]
        value_ref[owner_ref[e]] = quantize(fresh_ref[slot], older_ref[slot]).astype(jnp.bfloat16)


def encode(updated, trainer_base, sync_ids, owner_map):
    return pl.pallas_call(
        encode_kernel,
        in_specs=[pl.BlockSpec(memory_space=pl.ANY)] * 4,
        out_specs=pl.BlockSpec(memory_space=pltpu.VMEM),
        out_shape=jax.ShapeDtypeStruct((EXPERTS, ROWS, BLOCK), jnp.bfloat16),
        scratch_shapes=[
            pltpu.SMEM((EXPERTS,), jnp.int32),
            pltpu.SMEM((EXPERTS,), jnp.int32),
            pltpu.VMEM(updated.shape, jnp.bfloat16),
            pltpu.VMEM(updated.shape, jnp.bfloat16),
            pltpu.SemaphoreType.DMA((2, updated.shape[0])),
            pltpu.SemaphoreType.DMA((2,)),
        ],
        name="encode",
    )(sync_ids, owner_map, updated, trainer_base)


def swaps(zh):
    return (zh + 1) // 2 % 2


def exchange(values):
    groups = []
    for y in range(4):
        for group in range(2):
            groups.append(
                [(y * 2 + (group ^ swaps(s // 8))) * 32 + s for s in range(32)]
            )
    return lax.all_to_all(
        values, ("rollout", "shard"), split_axis=0, concat_axis=0, axis_index_groups=groups, tiled=True
    )


def shifted(block, dy=0, dz=0):
    pairs = []
    for y in range(4):
        for z in range(2):
            pairs.append((y * 2 + z, (y + dy) % 4 * 2 + (z + dz) % 2))
    return lax.ppermute(block, "rollout", pairs)


def column_of(k, band):
    rollout, zh = lax.axis_index("rollout"), lax.axis_index("shard") // 8
    dy, dz = MOVES[k]
    y = (rollout // 2 + dy + 4) % 4
    z = (rollout + dz + swaps(zh) + swaps(band)) % 2
    return pl.ds(pl.multiple_of((y * 2 + z) * BLOCK, BLOCK), BLOCK)


def cut(spans, low, high):
    found = []
    for n, (start, stop) in enumerate(spans):
        a, b = max(start, low), min(stop, high)
        if a < b:
            found.append((n, pl.ds(a - start, b - a), a, b - a))
    return found


def add_kernel(spans, base_ref, *refs):
    parts, (out_ref, rest_ref) = refs[:-2], refs[-2:]
    band = pl.program_id(0)
    for k in range(FIRST, 8):
        rest_ref[k - FIRST] = base_ref[:, column_of(k, band)]
    for n in range(4):

        @pl.when(band == n)
        def _():
            first = 0
            for k in range(FIRST):
                columns = column_of(k, band)
                for which, rows, a, size in cut(spans[k], n * BAND, (n + 1) * BAND):
                    at = pl.ds(a - n * BAND, size)
                    out_ref[at, columns] = base_ref[at, columns] + parts[first + which][rows, :]
                first += len(spans[k])


def add(base, spans, parts):
    rows = pl.BlockSpec((BAND, WIDTH), lambda i: (i, 0))
    return pl.pallas_call(
        functools.partial(add_kernel, spans),
        grid=(OWNED // BAND,),
        in_specs=[rows] + [pl.BlockSpec(memory_space=pltpu.VMEM)] * len(parts),
        out_specs=[rows, pl.BlockSpec((8 - FIRST, BAND, BLOCK), lambda i: (0, i, 0))],
        out_shape=[
            jax.ShapeDtypeStruct((OWNED, WIDTH), jnp.bfloat16),
            jax.ShapeDtypeStruct((8 - FIRST, OWNED, BLOCK), jnp.bfloat16),
        ],
        compiler_params=pltpu.CompilerParams(vmem_limit_bytes=12 * 2**20),
        cost_estimate=pl.CostEstimate(flops=OWNED * WIDTH, bytes_accessed=6 * OWNED * WIDTH, transcendentals=0),
        name="add",
    )(base, *parts)


def finish_kernel(spans, rest_ref, *refs):
    parts, (out_hbm, total_ref, sems) = refs[:-4], refs[-3:]
    copies = []
    first = 0
    for n in range(8 - FIRST):
        for band in range(4):
            for which, rows, a, size in cut(spans[n], band * BAND, (band + 1) * BAND):
                total_ref[n, pl.ds(a, size), :] = rest_ref[n, pl.ds(a, size), :] + parts[first + which][rows, :]
            rows = pl.ds(band * BAND, BAND)
            to = out_hbm.at[rows, column_of(n + FIRST, band)]
            copies.append(pltpu.make_async_copy(total_ref.at[n, rows], to, sems.at[n, band]))
            copies[-1].start()
        first += len(spans[n])
    for copy in copies:
        copy.wait()


def finish(rest, spans, parts, made):
    whole = pl.BlockSpec(memory_space=pltpu.VMEM)
    return pl.pallas_call(
        functools.partial(finish_kernel, spans),
        in_specs=[whole] * (1 + len(parts)) + [pl.BlockSpec(memory_space=pl.ANY)],
        out_specs=pl.BlockSpec(memory_space=pl.ANY),
        out_shape=jax.ShapeDtypeStruct((OWNED, WIDTH), jnp.bfloat16),
        scratch_shapes=[pltpu.VMEM((8 - FIRST, OWNED, BLOCK), jnp.bfloat16), pltpu.SemaphoreType.DMA((8 - FIRST, 4))],
        input_output_aliases={1 + len(parts): 0},
        compiler_params=pltpu.CompilerParams(vmem_limit_bytes=8 * 2**20),
        name="finish",
    )(rest, *parts, made)


def gather(own):
    own_a, own_b = own[:SPLIT], own[SPLIT:]
    beside_a, beside_b = shifted(own_a, dz=1), shifted(own_b, dz=1)
    below_a, above_b = shifted(own_a, dy=1), shifted(own_b, dy=-1)
    below_b, above_a = shifted(own_b, dy=1), shifted(own_a, dy=-1)
    bb_a, ba_b = shifted(beside_a, dy=1), shifted(beside_b, dy=-1)
    far_a, far_b = shifted(below_a, dy=1), shifted(above_b, dy=-1)
    bb_b, ba_a = shifted(below_b, dz=1), shifted(above_a, dz=1)
    fz_a, fz_b = shifted(bb_a, dy=1), shifted(ba_b, dy=-1)
    parts = [[own_a, own_b], [below_a, below_b], [above_a, above_b], [beside_a, beside_b], [far_a, far_b], [bb_a, bb_b], [ba_a, ba_b], [fz_a, fz_b]]
    spans = []
    for pieces in parts:
        ends = [sum(piece.shape[0] for piece in pieces[:n]) for n in range(len(pieces) + 1)]
        spans.append(list(zip(ends[:-1], ends[1:])))
    return parts, spans


def per_device(updated, trainer_base, rollout_base, sync_ids, owner_map):
    values = encode(updated, trainer_base, sync_ids, owner_map).reshape(32, PIECE, BLOCK)
    parts, spans = gather(exchange(values).reshape(OWNED, BLOCK))
    flat = lambda some: [piece for pieces in some for piece in pieces]
    made, rest = add(rollout_base[0], spans[:FIRST], flat(parts[:FIRST]))
    return finish(rest, spans[FIRST:], flat(parts[FIRST:]), made)[None]


def solution(mesh):
    return jax.shard_map(
        per_device,
        mesh=mesh,
        in_specs=(
            P(None, "shard", "rollout"),
            P(None, "shard", "rollout"),
            P("shard", None, None),
            P(),
            P(),
        ),
        out_specs=P("shard", None, None),
        check_vma=False,
    )
```

```python
import functools

import jax
import jax.numpy as jnp
from jax import lax
from jax.experimental import pallas as pl
from jax.experimental.pallas import tpu as pltpu
from jax.sharding import PartitionSpec as P

EXPERTS = 8
ROWS = 224
BLOCK = 128
PIECE = 56
OWNED = 1792
WIDTH = 1024
BAND = 448
SPLIT = 896
FIRST = 5
MOVES = [(0, 0), (-1, 0), (1, 0), (0, 1), (2, 0), (-1, 1), (1, 1), (2, 1)]


def floor_power(magnitude):
    spread = magnitude * (2.0**23 + 1.0)
    power = spread - (spread - magnitude)
    return jnp.where(power > magnitude, power * 0.5, power)


def quantize(fresh, older):
    delta = fresh.astype(jnp.float32) - older.astype(jnp.float32)
    magnitude = jnp.abs(delta)
    largest = jnp.max(magnitude, axis=-1, keepdims=True)
    power = floor_power(largest)
    scale = jnp.where(largest > 1.75 * power, power * 2.0**-7, power * 2.0**-8)
    scale = jnp.maximum(scale, 2.0**-24)
    binade = jnp.maximum(floor_power(magnitude), scale * 2.0**-6)
    shift = binade * (1.5 * 2.0**20)
    rounded = (magnitude + shift) - shift
    tie = (magnitude - rounded) >= binade * 2.0**-4
    rounded = jnp.where(tie, rounded + binade * 2.0**-3, rounded)
    return jnp.where(delta < 0.0, -rounded, rounded)


def encode_kernel(ids_hbm, owner_hbm, fresh_hbm, older_hbm, value_ref, ids_ref, owner_ref, fresh_ref, older_ref, sems, few):
    ids = pltpu.make_async_copy(ids_hbm, ids_ref, few.at[0])
    owner = pltpu.make_async_copy(owner_hbm, owner_ref, few.at[1])
    ids.start()
    owner.start()
    slots = fresh_ref.shape[0]
    copies = []
    for slot in range(slots):
        fresh = pltpu.make_async_copy(fresh_hbm.at[slot], fresh_ref.at[slot], sems.at[0, slot])
        older = pltpu.make_async_copy(older_hbm.at[slot], older_ref.at[slot], sems.at[1, slot])
        fresh.start()
        older.start()
        copies += [fresh, older]
    ids.wait()
    owner.wait()
    for copy in copies:
        copy.wait()

    @pl.loop(0, EXPERTS)
    def _(e):
        slot = ids_ref[e]
        value_ref[owner_ref[e]] = quantize(fresh_ref[slot], older_ref[slot]).astype(jnp.bfloat16)


def encode(updated, trainer_base, sync_ids, owner_map):
    return pl.pallas_call(
        encode_kernel,
        in_specs=[pl.BlockSpec(memory_space=pl.ANY)] * 4,
        out_specs=pl.BlockSpec(memory_space=pltpu.VMEM),
        out_shape=jax.ShapeDtypeStruct((EXPERTS, ROWS, BLOCK), jnp.bfloat16),
        scratch_shapes=[
            pltpu.SMEM((EXPERTS,), jnp.int32),
            pltpu.SMEM((EXPERTS,), jnp.int32),
            pltpu.VMEM(updated.shape, jnp.bfloat16),
            pltpu.VMEM(updated.shape, jnp.bfloat16),
            pltpu.SemaphoreType.DMA((2, updated.shape[0])),
            pltpu.SemaphoreType.DMA((2,)),
        ],
        name="encode",
    )(sync_ids, owner_map, updated, trainer_base)


def swaps(zh):
    return (zh + 1) // 2 % 2


def exchange(values):
    groups = []
    for y in range(4):
        for group in range(2):
            groups.append(
                [(y * 2 + (group ^ swaps(s // 8))) * 32 + s for s in range(32)]
            )
    return lax.all_to_all(
        values, ("rollout", "shard"), split_axis=0, concat_axis=0, axis_index_groups=groups, tiled=True
    )


def shifted(block, dy=0, dz=0):
    pairs = []
    for y in range(4):
        for z in range(2):
            pairs.append((y * 2 + z, (y + dy) % 4 * 2 + (z + dz) % 2))
    return lax.ppermute(block, "rollout", pairs)


def column_of(k, band):
    rollout, zh = lax.axis_index("rollout"), lax.axis_index("shard") // 8
    dy, dz = MOVES[k]
    y = (rollout // 2 + dy + 4) % 4
    z = (rollout + dz + swaps(zh) + swaps(band)) % 2
    return pl.ds(pl.multiple_of((y * 2 + z) * BLOCK, BLOCK), BLOCK)


def cut(spans, low, high):
    found = []
    for n, (start, stop) in enumerate(spans):
        a, b = max(start, low), min(stop, high)
        if a < b:
            found.append((n, pl.ds(a - start, b - a), a, b - a))
    return found


def add_kernel(spans, base_ref, *refs):
    parts, (out_ref, rest_ref) = refs[:-2], refs[-2:]
    band = pl.program_id(0)
    for k in range(FIRST, 8):
        rest_ref[k - FIRST] = base_ref[:, column_of(k, band)]
    for n in range(4):

        @pl.when(band == n)
        def _():
            first = 0
            for k in range(FIRST):
                columns = column_of(k, band)
                for which, rows, a, size in cut(spans[k], n * BAND, (n + 1) * BAND):
                    at = pl.ds(a - n * BAND, size)
                    out_ref[at, columns] = base_ref[at, columns] + parts[first + which][rows, :]
                first += len(spans[k])


def add(base, spans, parts):
    rows = pl.BlockSpec((BAND, WIDTH), lambda i: (i, 0))
    return pl.pallas_call(
        functools.partial(add_kernel, spans),
        grid=(OWNED // BAND,),
        in_specs=[rows] + [pl.BlockSpec(memory_space=pltpu.VMEM)] * len(parts),
        out_specs=[rows, pl.BlockSpec((8 - FIRST, BAND, BLOCK), lambda i: (0, i, 0))],
        out_shape=[
            jax.ShapeDtypeStruct((OWNED, WIDTH), jnp.bfloat16),
            jax.ShapeDtypeStruct((8 - FIRST, OWNED, BLOCK), jnp.bfloat16),
        ],
        compiler_params=pltpu.CompilerParams(vmem_limit_bytes=12 * 2**20),
        cost_estimate=pl.CostEstimate(flops=OWNED * WIDTH, bytes_accessed=6 * OWNED * WIDTH, transcendentals=0),
        name="add",
    )(base, *parts)


def finish_kernel(spans, rest_ref, *refs):
    parts, (out_hbm, total_ref, sems) = refs[:-4], refs[-3:]
    copies = []
    first = 0
    for n in range(8 - FIRST):
        for band in range(4):
            for which, rows, a, size in cut(spans[n], band * BAND, (band + 1) * BAND):
                total_ref[n, pl.ds(a, size), :] = rest_ref[n, pl.ds(a, size), :] + parts[first + which][rows, :]
            rows = pl.ds(band * BAND, BAND)
            to = out_hbm.at[rows, column_of(n + FIRST, band)]
            copies.append(pltpu.make_async_copy(total_ref.at[n, rows], to, sems.at[n, band]))
            copies[-1].start()
        first += len(spans[n])
    for copy in copies:
        copy.wait()


def finish(rest, spans, parts, made):
    whole = pl.BlockSpec(memory_space=pltpu.VMEM)
    return pl.pallas_call(
        functools.partial(finish_kernel, spans),
        in_specs=[whole] * (1 + len(parts)) + [pl.BlockSpec(memory_space=pl.ANY)],
        out_specs=pl.BlockSpec(memory_space=pl.ANY),
        out_shape=jax.ShapeDtypeStruct((OWNED, WIDTH), jnp.bfloat16),
        scratch_shapes=[pltpu.VMEM((8 - FIRST, OWNED, BLOCK), jnp.bfloat16), pltpu.SemaphoreType.DMA((8 - FIRST, 4))],
        input_output_aliases={1 + len(parts): 0},
        compiler_params=pltpu.CompilerParams(vmem_limit_bytes=8 * 2**20),
        name="finish",
    )(rest, *parts, made)


def gather(own):
    own_a, own_b = own[:SPLIT], own[SPLIT:]
    below_a, above_b = shifted(own_a, dy=1), shifted(own_b, dy=-1)
    beside = shifted(own, dz=1)
    below_b, above_a = shifted(own_b, dy=1), shifted(own_a, dy=-1)
    far_a, far_b = shifted(below_a, dy=1), shifted(above_b, dy=-1)
    up, below_b = lax.optimization_barrier((beside, below_b))
    down, above_a = lax.optimization_barrier((beside, above_a))
    bb, ba = shifted(up, dy=1), shifted(down, dy=-1)
    fz_a, fz_b = shifted(far_a, dz=1), shifted(far_b, dz=1)
    parts = [[own_a, own_b], [below_a, below_b], [above_a, above_b], [beside], [far_a, far_b], [bb], [ba], [fz_a, fz_b]]
    spans = []
    for pieces in parts:
        ends = [sum(piece.shape[0] for piece in pieces[:n]) for n in range(len(pieces) + 1)]
        spans.append(list(zip(ends[:-1], ends[1:])))
    return parts, spans


def per_device(updated, trainer_base, rollout_base, sync_ids, owner_map):
    values = encode(updated, trainer_base, sync_ids, owner_map).reshape(32, PIECE, BLOCK)
    parts, spans = gather(exchange(values).reshape(OWNED, BLOCK))
    flat = lambda some: [piece for pieces in some for piece in pieces]
    made, rest = add(rollout_base[0], spans[:FIRST], flat(parts[:FIRST]))
    return finish(rest, spans[FIRST:], flat(parts[FIRST:]), made)[None]


def solution(mesh):
    return jax.shard_map(
        per_device,
        mesh=mesh,
        in_specs=(
            P(None, "shard", "rollout"),
            P(None, "shard", "rollout"),
            P("shard", None, None),
            P(),
            P(),
        ),
        out_specs=P("shard", None, None),
        check_vma=False,
    )
```

```python
import functools

import jax
import jax.numpy as jnp
from jax import lax
from jax.experimental import pallas as pl
from jax.experimental.pallas import tpu as pltpu
from jax.sharding import PartitionSpec as P

EXPERTS = 8
ROWS = 224
BLOCK = 128
PIECE = 56
OWNED = 1792
WIDTH = 1024
BAND = 448
SPLIT = 896
FIRST = 5
MOVES = [(0, 0), (-1, 0), (1, 0), (0, 1), (2, 0), (-1, 1), (1, 1), (2, 1)]


def floor_power(magnitude):
    spread = magnitude * (2.0**23 + 1.0)
    power = spread - (spread - magnitude)
    return jnp.where(power > magnitude, power * 0.5, power)


def quantize(fresh, older):
    delta = fresh.astype(jnp.float32) - older.astype(jnp.float32)
    magnitude = jnp.abs(delta)
    largest = jnp.max(magnitude, axis=-1, keepdims=True)
    power = floor_power(largest)
    scale = jnp.where(largest > 1.75 * power, power * 2.0**-7, power * 2.0**-8)
    scale = jnp.maximum(scale, 2.0**-24)
    binade = jnp.maximum(floor_power(magnitude), scale * 2.0**-6)
    shift = binade * (1.5 * 2.0**20)
    rounded = (magnitude + shift) - shift
    tie = (magnitude - rounded) >= binade * 2.0**-4
    rounded = jnp.where(tie, rounded + binade * 2.0**-3, rounded)
    return jnp.where(delta < 0.0, -rounded, rounded)


def encode_kernel(ids_hbm, owner_hbm, fresh_hbm, older_hbm, out_hbm, ids_ref, owner_ref, place_ref, fresh_ref, older_ref, value_ref, sems, few, sent):
    slots = fresh_ref.shape[0]
    ids = pltpu.make_async_copy(ids_hbm, ids_ref, few.at[0])
    owner = pltpu.make_async_copy(owner_hbm, owner_ref, few.at[1])
    ids.start()
    owner.start()
    copies = []
    for slot in range(slots):
        fresh = pltpu.make_async_copy(fresh_hbm.at[slot], fresh_ref.at[slot], sems.at[0, slot])
        older = pltpu.make_async_copy(older_hbm.at[slot], older_ref.at[slot], sems.at[1, slot])
        fresh.start()
        older.start()
        copies.append((fresh, older))
    for slot in range(slots):
        place_ref[slot] = -1
    ids.wait()
    owner.wait()
    for e in range(EXPERTS):
        place_ref[ids_ref[e]] = owner_ref[e]
    for slot, (fresh, older) in enumerate(copies):
        fresh.wait()
        older.wait()
        place = place_ref[slot]

        @pl.when(place >= 0)
        def _():
            value_ref[place] = quantize(fresh_ref[slot], older_ref[slot]).astype(jnp.bfloat16)
            pltpu.make_async_copy(value_ref.at[place], out_hbm.at[place], sent.at[place]).start()

    for e in range(EXPERTS):
        pltpu.make_async_copy(value_ref.at[e], out_hbm.at[e], sent.at[e]).wait()


def encode(updated, trainer_base, sync_ids, owner_map):
    slots = updated.shape[0]
    anywhere = pl.BlockSpec(memory_space=pl.ANY)
    return pl.pallas_call(
        encode_kernel,
        in_specs=[anywhere] * 4,
        out_specs=anywhere,
        out_shape=jax.ShapeDtypeStruct((EXPERTS, ROWS, BLOCK), jnp.bfloat16),
        scratch_shapes=[
            pltpu.SMEM((EXPERTS,), jnp.int32),
            pltpu.SMEM((EXPERTS,), jnp.int32),
            pltpu.SMEM((slots,), jnp.int32),
            pltpu.VMEM(updated.shape, jnp.bfloat16),
            pltpu.VMEM(updated.shape, jnp.bfloat16),
            pltpu.VMEM((EXPERTS, ROWS, BLOCK), jnp.bfloat16),
            pltpu.SemaphoreType.DMA((2, slots)),
            pltpu.SemaphoreType.DMA((2,)),
            pltpu.SemaphoreType.DMA((EXPERTS,)),
        ],
        name="encode",
    )(sync_ids, owner_map, updated, trainer_base)


def swaps(zh):
    return (zh + 1) // 2 % 2


def exchange(values):
    groups = []
    for y in range(4):
        for group in range(2):
            groups.append(
                [(y * 2 + (group ^ swaps(s // 8))) * 32 + s for s in range(32)]
            )
    return lax.all_to_all(
        values, ("rollout", "shard"), split_axis=0, concat_axis=0, axis_index_groups=groups, tiled=True
    )


def shifted(block, dy=0, dz=0):
    pairs = []
    for y in range(4):
        for z in range(2):
            pairs.append((y * 2 + z, (y + dy) % 4 * 2 + (z + dz) % 2))
    return lax.ppermute(block, "rollout", pairs)


def column_of(k, band):
    rollout, zh = lax.axis_index("rollout"), lax.axis_index("shard") // 8
    dy, dz = MOVES[k]
    y = (rollout // 2 + dy + 4) % 4
    z = (rollout + dz + swaps(zh) + swaps(band)) % 2
    return pl.ds(pl.multiple_of((y * 2 + z) * BLOCK, BLOCK), BLOCK)


def cut(spans, low, high):
    found = []
    for n, (start, stop) in enumerate(spans):
        a, b = max(start, low), min(stop, high)
        if a < b:
            found.append((n, pl.ds(a - start, b - a), a, b - a))
    return found


def add_kernel(spans, base_ref, *refs):
    parts, (out_ref, rest_ref) = refs[:-2], refs[-2:]
    band = pl.program_id(0)
    for k in range(FIRST, 8):
        rest_ref[k - FIRST] = base_ref[:, column_of(k, band)]
    for n in range(4):

        @pl.when(band == n)
        def _():
            first = 0
            for k in range(FIRST):
                columns = column_of(k, band)
                for which, rows, a, size in cut(spans[k], n * BAND, (n + 1) * BAND):
                    at = pl.ds(a - n * BAND, size)
                    out_ref[at, columns] = base_ref[at, columns] + parts[first + which][rows, :]
                first += len(spans[k])


def add(base, spans, parts):
    rows = pl.BlockSpec((BAND, WIDTH), lambda i: (i, 0))
    return pl.pallas_call(
        functools.partial(add_kernel, spans),
        grid=(OWNED // BAND,),
        in_specs=[rows] + [pl.BlockSpec(memory_space=pltpu.VMEM)] * len(parts),
        out_specs=[rows, pl.BlockSpec((8 - FIRST, BAND, BLOCK), lambda i: (0, i, 0))],
        out_shape=[
            jax.ShapeDtypeStruct((OWNED, WIDTH), jnp.bfloat16),
            jax.ShapeDtypeStruct((8 - FIRST, OWNED, BLOCK), jnp.bfloat16),
        ],
        compiler_params=pltpu.CompilerParams(vmem_limit_bytes=12 * 2**20),
        cost_estimate=pl.CostEstimate(flops=OWNED * WIDTH, bytes_accessed=6 * OWNED * WIDTH, transcendentals=0),
        name="add",
    )(base, *parts)


def finish_kernel(spans, rest_ref, *refs):
    parts, (out_hbm, total_ref, sems) = refs[:-4], refs[-3:]
    copies = []
    first = 0
    for n in range(8 - FIRST):
        for band in range(4):
            for which, rows, a, size in cut(spans[n], band * BAND, (band + 1) * BAND):
                total_ref[n, pl.ds(a, size), :] = rest_ref[n, pl.ds(a, size), :] + parts[first + which][rows, :]
            rows = pl.ds(band * BAND, BAND)
            to = out_hbm.at[rows, column_of(n + FIRST, band)]
            copies.append(pltpu.make_async_copy(total_ref.at[n, rows], to, sems.at[n, band]))
            copies[-1].start()
        first += len(spans[n])
    for copy in copies:
        copy.wait()


def finish(rest, spans, parts, made):
    whole = pl.BlockSpec(memory_space=pltpu.VMEM)
    return pl.pallas_call(
        functools.partial(finish_kernel, spans),
        in_specs=[whole] * (1 + len(parts)) + [pl.BlockSpec(memory_space=pl.ANY)],
        out_specs=pl.BlockSpec(memory_space=pl.ANY),
        out_shape=jax.ShapeDtypeStruct((OWNED, WIDTH), jnp.bfloat16),
        scratch_shapes=[pltpu.VMEM((8 - FIRST, OWNED, BLOCK), jnp.bfloat16), pltpu.SemaphoreType.DMA((8 - FIRST, 4))],
        input_output_aliases={1 + len(parts): 0},
        compiler_params=pltpu.CompilerParams(vmem_limit_bytes=8 * 2**20),
        name="finish",
    )(rest, *parts, made)


def gather(own):
    own_a, own_b = own[:SPLIT], own[SPLIT:]
    below_a, above_b = shifted(own_a, dy=1), shifted(own_b, dy=-1)
    beside = shifted(own, dz=1)
    below_b, above_a = shifted(own_b, dy=1), shifted(own_a, dy=-1)
    far_a, far_b = shifted(below_a, dy=1), shifted(above_b, dy=-1)
    up, below_b = lax.optimization_barrier((beside, below_b))
    down, above_a = lax.optimization_barrier((beside, above_a))
    bb, ba = shifted(up, dy=1), shifted(down, dy=-1)
    fz_a, fz_b = shifted(far_a, dz=1), shifted(far_b, dz=1)
    parts = [[own_a, own_b], [below_a, below_b], [above_a, above_b], [beside], [far_a, far_b], [bb], [ba], [fz_a, fz_b]]
    spans = []
    for pieces in parts:
        ends = [sum(piece.shape[0] for piece in pieces[:n]) for n in range(len(pieces) + 1)]
        spans.append(list(zip(ends[:-1], ends[1:])))
    return parts, spans


def per_device(updated, trainer_base, rollout_base, sync_ids, owner_map):
    values = encode(updated, trainer_base, sync_ids, owner_map).reshape(32, PIECE, BLOCK)
    parts, spans = gather(exchange(values).reshape(OWNED, BLOCK))
    flat = lambda some: [piece for pieces in some for piece in pieces]
    made, rest = add(rollout_base[0], spans[:FIRST], flat(parts[:FIRST]))
    return finish(rest, spans[FIRST:], flat(parts[FIRST:]), made)[None]


def solution(mesh):
    return jax.shard_map(
        per_device,
        mesh=mesh,
        in_specs=(
            P(None, "shard", "rollout"),
            P(None, "shard", "rollout"),
            P("shard", None, None),
            P(),
            P(),
        ),
        out_specs=P("shard", None, None),
        check_vma=False,
    )
```

```python
import functools

import jax
import jax.numpy as jnp
from jax import lax
from jax.experimental import pallas as pl
from jax.experimental.pallas import tpu as pltpu
from jax.sharding import PartitionSpec as P

EXPERTS = 8
ROWS = 224
BLOCK = 128
PIECE = 56
OWNED = 1792
WIDTH = 1024
BAND = 448
SPLIT = 896
FIRST = 5
MOVES = [(0, 0), (1, 0), (0, 1), (-1, 0), (2, 0), (-1, 1), (1, 1), (2, 1)]


def floor_power(magnitude):
    spread = magnitude * (2.0**23 + 1.0)
    power = spread - (spread - magnitude)
    return jnp.where(power > magnitude, power * 0.5, power)


def quantize(fresh, older):
    delta = fresh.astype(jnp.float32) - older.astype(jnp.float32)
    magnitude = jnp.abs(delta)
    largest = jnp.max(magnitude, axis=-1, keepdims=True)
    power = floor_power(largest)
    scale = jnp.where(largest > 1.75 * power, power * 2.0**-7, power * 2.0**-8)
    scale = jnp.maximum(scale, 2.0**-24)
    binade = jnp.maximum(floor_power(magnitude), scale * 2.0**-6)
    shift = binade * (1.5 * 2.0**20)
    rounded = (magnitude + shift) - shift
    tie = (magnitude - rounded) >= binade * 2.0**-4
    rounded = jnp.where(tie, rounded + binade * 2.0**-3, rounded)
    return jnp.where(delta < 0.0, -rounded, rounded)


def encode_kernel(ids_hbm, owner_hbm, fresh_hbm, older_hbm, out_hbm, ids_ref, owner_ref, place_ref, fresh_ref, older_ref, value_ref, sems, few, sent):
    slots = fresh_ref.shape[0]
    ids = pltpu.make_async_copy(ids_hbm, ids_ref, few.at[0])
    owner = pltpu.make_async_copy(owner_hbm, owner_ref, few.at[1])
    ids.start()
    owner.start()
    copies = []
    for slot in range(slots):
        fresh = pltpu.make_async_copy(fresh_hbm.at[slot], fresh_ref.at[slot], sems.at[0, slot])
        older = pltpu.make_async_copy(older_hbm.at[slot], older_ref.at[slot], sems.at[1, slot])
        fresh.start()
        older.start()
        copies.append((fresh, older))
    for slot in range(slots):
        place_ref[slot] = -1
    ids.wait()
    owner.wait()
    for e in range(EXPERTS):
        place_ref[ids_ref[e]] = owner_ref[e]
    for slot, (fresh, older) in enumerate(copies):
        fresh.wait()
        older.wait()
        place = place_ref[slot]

        @pl.when(place >= 0)
        def _():
            value_ref[place] = quantize(fresh_ref[slot], older_ref[slot]).astype(jnp.bfloat16)
            pltpu.make_async_copy(value_ref.at[place], out_hbm.at[place], sent.at[place]).start()

    for e in range(EXPERTS):
        pltpu.make_async_copy(value_ref.at[e], out_hbm.at[e], sent.at[e]).wait()


def encode(updated, trainer_base, sync_ids, owner_map):
    slots = updated.shape[0]
    anywhere = pl.BlockSpec(memory_space=pl.ANY)
    return pl.pallas_call(
        encode_kernel,
        in_specs=[anywhere] * 4,
        out_specs=anywhere,
        out_shape=jax.ShapeDtypeStruct((EXPERTS, ROWS, BLOCK), jnp.bfloat16),
        scratch_shapes=[
            pltpu.SMEM((EXPERTS,), jnp.int32),
            pltpu.SMEM((EXPERTS,), jnp.int32),
            pltpu.SMEM((slots,), jnp.int32),
            pltpu.VMEM(updated.shape, jnp.bfloat16),
            pltpu.VMEM(updated.shape, jnp.bfloat16),
            pltpu.VMEM((EXPERTS, ROWS, BLOCK), jnp.bfloat16),
            pltpu.SemaphoreType.DMA((2, slots)),
            pltpu.SemaphoreType.DMA((2,)),
            pltpu.SemaphoreType.DMA((EXPERTS,)),
        ],
        name="encode",
    )(sync_ids, owner_map, updated, trainer_base)


def swaps(zh):
    return (zh + 1) // 2 % 2


def exchange(values):
    groups = []
    for y in range(4):
        for group in range(2):
            groups.append(
                [(y * 2 + (group ^ swaps(s // 8))) * 32 + s for s in range(32)]
            )
    return lax.all_to_all(
        values, ("rollout", "shard"), split_axis=0, concat_axis=0, axis_index_groups=groups, tiled=True
    )


def shifted(block, dy=0, dz=0):
    pairs = []
    for y in range(4):
        for z in range(2):
            pairs.append((y * 2 + z, (y + dy) % 4 * 2 + (z + dz) % 2))
    return lax.ppermute(block, "rollout", pairs)


def column_of(k, band):
    rollout, zh = lax.axis_index("rollout"), lax.axis_index("shard") // 8
    dy, dz = MOVES[k]
    y = (rollout // 2 + dy + 4) % 4
    z = (rollout + dz + swaps(zh) + swaps(band)) % 2
    return pl.ds(pl.multiple_of((y * 2 + z) * BLOCK, BLOCK), BLOCK)


def cut(spans, low, high):
    found = []
    for n, (start, stop) in enumerate(spans):
        a, b = max(start, low), min(stop, high)
        if a < b:
            found.append((n, pl.ds(a - start, b - a), a, b - a))
    return found


def add_kernel(spans, base_ref, *refs):
    parts, (out_ref, rest_ref) = refs[:-2], refs[-2:]
    band = pl.program_id(0)
    for k in range(FIRST, 8):
        rest_ref[k - FIRST] = base_ref[:, column_of(k, band)]
    for n in range(4):

        @pl.when(band == n)
        def _():
            first = 0
            for k in range(FIRST):
                columns = column_of(k, band)
                for which, rows, a, size in cut(spans[k], n * BAND, (n + 1) * BAND):
                    at = pl.ds(a - n * BAND, size)
                    out_ref[at, columns] = base_ref[at, columns] + parts[first + which][rows, :]
                first += len(spans[k])


def add(base, spans, parts):
    rows = pl.BlockSpec((BAND, WIDTH), lambda i: (i, 0))
    return pl.pallas_call(
        functools.partial(add_kernel, spans),
        grid=(OWNED // BAND,),
        in_specs=[rows] + [pl.BlockSpec(memory_space=pltpu.VMEM)] * len(parts),
        out_specs=[rows, pl.BlockSpec((8 - FIRST, BAND, BLOCK), lambda i: (0, i, 0))],
        out_shape=[
            jax.ShapeDtypeStruct((OWNED, WIDTH), jnp.bfloat16),
            jax.ShapeDtypeStruct((8 - FIRST, OWNED, BLOCK), jnp.bfloat16),
        ],
        compiler_params=pltpu.CompilerParams(vmem_limit_bytes=12 * 2**20),
        cost_estimate=pl.CostEstimate(flops=OWNED * WIDTH, bytes_accessed=6 * OWNED * WIDTH, transcendentals=0),
        name="add",
    )(base, *parts)


def finish_kernel(spans, rest_ref, *refs):
    parts, (out_hbm, total_ref, sems) = refs[:-4], refs[-3:]
    copies = []
    first = 0
    for n in range(8 - FIRST):
        for band in range(4):
            for which, rows, a, size in cut(spans[n], band * BAND, (band + 1) * BAND):
                total_ref[n, pl.ds(a, size), :] = rest_ref[n, pl.ds(a, size), :] + parts[first + which][rows, :]
            rows = pl.ds(band * BAND, BAND)
            to = out_hbm.at[rows, column_of(n + FIRST, band)]
            copies.append(pltpu.make_async_copy(total_ref.at[n, rows], to, sems.at[n, band]))
            copies[-1].start()
        first += len(spans[n])
    for copy in copies:
        copy.wait()


def finish(rest, spans, parts, made):
    whole = pl.BlockSpec(memory_space=pltpu.VMEM)
    return pl.pallas_call(
        functools.partial(finish_kernel, spans),
        in_specs=[whole] * (1 + len(parts)) + [pl.BlockSpec(memory_space=pl.ANY)],
        out_specs=pl.BlockSpec(memory_space=pl.ANY),
        out_shape=jax.ShapeDtypeStruct((OWNED, WIDTH), jnp.bfloat16),
        scratch_shapes=[pltpu.VMEM((8 - FIRST, OWNED, BLOCK), jnp.bfloat16), pltpu.SemaphoreType.DMA((8 - FIRST, 4))],
        input_output_aliases={1 + len(parts): 0},
        compiler_params=pltpu.CompilerParams(vmem_limit_bytes=8 * 2**20),
        name="finish",
    )(rest, *parts, made)


def join_kernel(a_ref, b_ref, below_ref, above_ref, whole_ref):
    whole_ref[:SPLIT] = a_ref[...]
    whole_ref[SPLIT:] = b_ref[...]


def joined(a, b, below, above):
    block = pl.BlockSpec(memory_space=pltpu.VMEM)
    anywhere = pl.BlockSpec(memory_space=pl.ANY)
    return pl.pallas_call(
        join_kernel,
        in_specs=[block, block, anywhere, anywhere],
        out_specs=block,
        out_shape=jax.ShapeDtypeStruct((OWNED, BLOCK), jnp.bfloat16),
        compiler_params=pltpu.CompilerParams(vmem_limit_bytes=2 * 2**20),
        name="joined",
    )(a, b, below, above)


def gather(own):
    own_a, own_b = own[:SPLIT], own[SPLIT:]
    below_a, above_b = shifted(own_a, dy=1), shifted(own_b, dy=-1)
    beside_a, beside_b = shifted(own_a, dz=1), shifted(own_b, dz=1)
    below_b, above_a = shifted(own_b, dy=1), shifted(own_a, dy=-1)
    far_a, far_b = shifted(below_a, dy=1), shifted(above_b, dy=-1)
    beside = joined(beside_a, beside_b, below_b, above_a)
    bb, ba = shifted(beside, dy=1), shifted(beside, dy=-1)
    fz_a, fz_b = shifted(far_a, dz=1), shifted(far_b, dz=1)
    parts = [
        [(own_a, 0), (own_b, SPLIT)],
        [(above_a, 0), (above_b, SPLIT)],
        [(beside, 0)],
        [(below_a, 0), (below_b, SPLIT)],
        [(far_a, 0), (far_b, SPLIT)],
        [(bb, 0)],
        [(ba, 0)],
        [(fz_a, 0), (fz_b, SPLIT)],
    ]
    spans = [[(start, start + piece.shape[0]) for piece, start in pieces] for pieces in parts]
    return [[piece for piece, _ in pieces] for pieces in parts], spans


def per_device(updated, trainer_base, rollout_base, sync_ids, owner_map):
    values = encode(updated, trainer_base, sync_ids, owner_map).reshape(32, PIECE, BLOCK)
    parts, spans = gather(exchange(values).reshape(OWNED, BLOCK))
    flat = lambda some: [piece for pieces in some for piece in pieces]
    made, rest = add(rollout_base[0], spans[:FIRST], flat(parts[:FIRST]))
    return finish(rest, spans[FIRST:], flat(parts[FIRST:]), made)[None]


def solution(mesh):
    return jax.shard_map(
        per_device,
        mesh=mesh,
        in_specs=(
            P(None, "shard", "rollout"),
            P(None, "shard", "rollout"),
            P("shard", None, None),
            P(),
            P(),
        ),
        out_specs=P("shard", None, None),
        check_vma=False,
    )
```

```python
import functools

import jax
import jax.numpy as jnp
from jax import lax
from jax.experimental import pallas as pl
from jax.experimental.pallas import tpu as pltpu
from jax.sharding import PartitionSpec as P

EXPERTS = 8
ROWS = 224
BLOCK = 128
PIECE = 56
OWNED = 1792
WIDTH = 1024
BAND = 448
SPLIT = 896
FIRST = 5
MOVES = [(0, 0), (1, 0), (0, 1), (-1, 0), (2, 0), (1, 1), (-1, 1), (2, 1)]


def leading(magnitude):
    spread = magnitude * (2.0**23 + 1.0)
    return spread - (spread - magnitude)


def quantize(fresh, older):
    delta = fresh.astype(jnp.float32) - older.astype(jnp.float32)
    magnitude = jnp.abs(delta)
    largest = jnp.max(magnitude, axis=-1, keepdims=True)
    power = leading(largest)
    least = jnp.where(largest > 0.875 * power, power * 2.0**-14, power * 2.0**-15)
    least = jnp.maximum(least, 2.0**-30)
    power = leading(magnitude)
    binade = jnp.maximum(jnp.where(power > magnitude, power * 0.5, power), least)
    shift = binade * (1.5 * 2.0**20)
    rounded = (delta + shift) - shift
    error = delta - rounded
    short = (magnitude - jnp.abs(rounded)) >= binade * 2.0**-4
    return jnp.where(short, delta + error, rounded)


def encode_kernel(ids_hbm, owner_hbm, fresh_hbm, older_hbm, out_hbm, ids_ref, owner_ref, place_ref, fresh_ref, older_ref, value_ref, sems, few, sent):
    slots = fresh_ref.shape[0]
    ids = pltpu.make_async_copy(ids_hbm, ids_ref, few.at[0])
    owner = pltpu.make_async_copy(owner_hbm, owner_ref, few.at[1])
    ids.start()
    owner.start()
    copies = []
    for slot in range(slots):
        fresh = pltpu.make_async_copy(fresh_hbm.at[slot], fresh_ref.at[slot], sems.at[0, slot])
        older = pltpu.make_async_copy(older_hbm.at[slot], older_ref.at[slot], sems.at[1, slot])
        fresh.start()
        older.start()
        copies.append((fresh, older))
    for slot in range(slots):
        place_ref[slot] = -1
    ids.wait()
    owner.wait()
    for e in range(EXPERTS):
        place_ref[ids_ref[e]] = owner_ref[e]
    for slot, (fresh, older) in enumerate(copies):
        fresh.wait()
        older.wait()
        place = place_ref[slot]

        @pl.when(place >= 0)
        def _():
            value_ref[place] = quantize(fresh_ref[slot], older_ref[slot]).astype(jnp.bfloat16)
            pltpu.make_async_copy(value_ref.at[place], out_hbm.at[place], sent.at[place]).start()

    for e in range(EXPERTS):
        pltpu.make_async_copy(value_ref.at[e], out_hbm.at[e], sent.at[e]).wait()


def encode(updated, trainer_base, sync_ids, owner_map):
    slots = updated.shape[0]
    anywhere = pl.BlockSpec(memory_space=pl.ANY)
    return pl.pallas_call(
        encode_kernel,
        in_specs=[anywhere] * 4,
        out_specs=anywhere,
        out_shape=jax.ShapeDtypeStruct((EXPERTS, ROWS, BLOCK), jnp.bfloat16),
        scratch_shapes=[
            pltpu.SMEM((EXPERTS,), jnp.int32),
            pltpu.SMEM((EXPERTS,), jnp.int32),
            pltpu.SMEM((slots,), jnp.int32),
            pltpu.VMEM(updated.shape, jnp.bfloat16),
            pltpu.VMEM(updated.shape, jnp.bfloat16),
            pltpu.VMEM((EXPERTS, ROWS, BLOCK), jnp.bfloat16),
            pltpu.SemaphoreType.DMA((2, slots)),
            pltpu.SemaphoreType.DMA((2,)),
            pltpu.SemaphoreType.DMA((EXPERTS,)),
        ],
        name="encode",
    )(sync_ids, owner_map, updated, trainer_base)


def swaps(zh):
    return (zh + 1) // 2 % 2


def exchange(values):
    groups = []
    for y in range(4):
        for group in range(2):
            groups.append(
                [(y * 2 + (group ^ swaps(s // 8))) * 32 + s for s in range(32)]
            )
    return lax.all_to_all(
        values, ("rollout", "shard"), split_axis=0, concat_axis=0, axis_index_groups=groups, tiled=True
    )


def shifted(block, dy=0, dz=0):
    pairs = []
    for y in range(4):
        for z in range(2):
            pairs.append((y * 2 + z, (y + dy) % 4 * 2 + (z + dz) % 2))
    return lax.ppermute(block, "rollout", pairs)


def column_of(k, band):
    rollout, zh = lax.axis_index("rollout"), lax.axis_index("shard") // 8
    dy, dz = MOVES[k]
    y = (rollout // 2 + dy + 4) % 4
    z = (rollout + dz + swaps(zh) + swaps(band)) % 2
    return pl.ds(pl.multiple_of((y * 2 + z) * BLOCK, BLOCK), BLOCK)


def cut(spans, low, high):
    found = []
    for n, (start, stop) in enumerate(spans):
        a, b = max(start, low), min(stop, high)
        if a < b:
            found.append((n, pl.ds(a - start, b - a), a, b - a))
    return found


def add_kernel(spans, base_ref, *refs):
    parts, (out_ref, rest_ref) = refs[:-2], refs[-2:]
    band = pl.program_id(0)
    for k in range(FIRST, 8):
        rest_ref[k - FIRST] = base_ref[:, column_of(k, band)]
    for n in range(4):

        @pl.when(band == n)
        def _():
            first = 0
            for k in range(FIRST):
                columns = column_of(k, band)
                for which, rows, a, size in cut(spans[k], n * BAND, (n + 1) * BAND):
                    at = pl.ds(a - n * BAND, size)
                    out_ref[at, columns] = base_ref[at, columns] + parts[first + which][rows, :]
                first += len(spans[k])


def add(base, spans, parts):
    rows = pl.BlockSpec((BAND, WIDTH), lambda i: (i, 0))
    return pl.pallas_call(
        functools.partial(add_kernel, spans),
        grid=(OWNED // BAND,),
        in_specs=[rows] + [pl.BlockSpec(memory_space=pltpu.VMEM)] * len(parts),
        out_specs=[rows, pl.BlockSpec((8 - FIRST, BAND, BLOCK), lambda i: (0, i, 0))],
        out_shape=[
            jax.ShapeDtypeStruct((OWNED, WIDTH), jnp.bfloat16),
            jax.ShapeDtypeStruct((8 - FIRST, OWNED, BLOCK), jnp.bfloat16),
        ],
        compiler_params=pltpu.CompilerParams(vmem_limit_bytes=12 * 2**20),
        cost_estimate=pl.CostEstimate(flops=OWNED * WIDTH, bytes_accessed=6 * OWNED * WIDTH, transcendentals=0),
        name="add",
    )(base, *parts)


def finish_kernel(spans, rest_ref, *refs):
    parts, (out_hbm, total_ref, sems) = refs[:-4], refs[-3:]
    copies = []
    first = 0
    for n in range(8 - FIRST):
        for band in range(4):
            for which, rows, a, size in cut(spans[n], band * BAND, (band + 1) * BAND):
                total_ref[n, pl.ds(a, size), :] = rest_ref[n, pl.ds(a, size), :] + parts[first + which][rows, :]
            rows = pl.ds(band * BAND, BAND)
            to = out_hbm.at[rows, column_of(n + FIRST, band)]
            copies.append(pltpu.make_async_copy(total_ref.at[n, rows], to, sems.at[n, band]))
            copies[-1].start()
        first += len(spans[n])
    for copy in copies:
        copy.wait()


def finish(rest, spans, parts, made):
    whole = pl.BlockSpec(memory_space=pltpu.VMEM)
    return pl.pallas_call(
        functools.partial(finish_kernel, spans),
        in_specs=[whole] * (1 + len(parts)) + [pl.BlockSpec(memory_space=pl.ANY)],
        out_specs=pl.BlockSpec(memory_space=pl.ANY),
        out_shape=jax.ShapeDtypeStruct((OWNED, WIDTH), jnp.bfloat16),
        scratch_shapes=[pltpu.VMEM((8 - FIRST, OWNED, BLOCK), jnp.bfloat16), pltpu.SemaphoreType.DMA((8 - FIRST, 4))],
        input_output_aliases={1 + len(parts): 0},
        compiler_params=pltpu.CompilerParams(vmem_limit_bytes=8 * 2**20),
        name="finish",
    )(rest, *parts, made)


def join_kernel(a_ref, b_ref, below_ref, above_ref, whole_ref):
    whole_ref[:SPLIT] = a_ref[...]
    whole_ref[SPLIT:] = b_ref[...]


def joined(a, b, below, above):
    block = pl.BlockSpec(memory_space=pltpu.VMEM)
    anywhere = pl.BlockSpec(memory_space=pl.ANY)
    return pl.pallas_call(
        join_kernel,
        in_specs=[block, block, anywhere, anywhere],
        out_specs=block,
        out_shape=jax.ShapeDtypeStruct((OWNED, BLOCK), jnp.bfloat16),
        compiler_params=pltpu.CompilerParams(vmem_limit_bytes=2 * 2**20),
        name="joined",
    )(a, b, below, above)


def gather(own):
    own_a, own_b = own[:SPLIT], own[SPLIT:]
    below_a, above_b = shifted(own_a, dy=1), shifted(own_b, dy=-1)
    beside_a, beside_b = shifted(own_a, dz=1), shifted(own_b, dz=1)
    below_b, above_a = shifted(own_b, dy=1), shifted(own_a, dy=-1)
    far_a, far_b = shifted(below_a, dy=1), shifted(above_b, dy=-1)
    beside = joined(beside_a, beside_b, below_b, above_a)
    bb, ba = shifted(beside, dy=1), shifted(beside, dy=-1)
    fz_a, fz_b = shifted(far_a, dz=1), shifted(far_b, dz=1)
    parts = [
        [(own_a, 0), (own_b, SPLIT)],
        [(above_a, 0), (above_b, SPLIT)],
        [(beside, 0)],
        [(below_a, 0), (below_b, SPLIT)],
        [(far_a, 0), (far_b, SPLIT)],
        [(ba, 0)],
        [(bb, 0)],
        [(fz_a, 0), (fz_b, SPLIT)],
    ]
    spans = [[(start, start + piece.shape[0]) for piece, start in pieces] for pieces in parts]
    return [[piece for piece, _ in pieces] for pieces in parts], spans


def per_device(updated, trainer_base, rollout_base, sync_ids, owner_map):
    values = encode(updated, trainer_base, sync_ids, owner_map).reshape(32, PIECE, BLOCK)
    parts, spans = gather(exchange(values).reshape(OWNED, BLOCK))
    flat = lambda some: [piece for pieces in some for piece in pieces]
    made, rest = add(rollout_base[0], spans[:FIRST], flat(parts[:FIRST]))
    return finish(rest, spans[FIRST:], flat(parts[FIRST:]), made)[None]


def solution(mesh):
    return jax.shard_map(
        per_device,
        mesh=mesh,
        in_specs=(
            P(None, "shard", "rollout"),
            P(None, "shard", "rollout"),
            P("shard", None, None),
            P(),
            P(),
        ),
        out_specs=P("shard", None, None),
        check_vma=False,
    )
```

```python
import functools

import jax
import jax.numpy as jnp
from jax import lax
from jax.experimental import pallas as pl
from jax.experimental.pallas import tpu as pltpu
from jax.sharding import PartitionSpec as P

EXPERTS = 8
ROWS = 224
BLOCK = 128
PIECE = 56
OWNED = 1792
WIDTH = 1024
BAND = 448
SPLIT = 896
EDGE = 256
FIRST = 5
MOVES = [(0, 0), (1, 0), (0, 1), (-1, 0), (2, 0), (1, 1), (-1, 1), (2, 1)]


def leading(magnitude):
    spread = magnitude * (2.0**23 + 1.0)
    return spread - (spread - magnitude)


def quantize(fresh, older):
    delta = fresh.astype(jnp.float32) - older.astype(jnp.float32)
    magnitude = jnp.abs(delta)
    largest = jnp.max(magnitude, axis=-1, keepdims=True)
    power = leading(largest)
    least = jnp.where(largest > 0.875 * power, power * 2.0**-14, power * 2.0**-15)
    least = jnp.maximum(least, 2.0**-30)
    power = leading(magnitude)
    binade = jnp.maximum(jnp.where(power > magnitude, power * 0.5, power), least)
    shift = binade * (1.5 * 2.0**20)
    rounded = (delta + shift) - shift
    error = delta - rounded
    short = (magnitude - jnp.abs(rounded)) >= binade * 2.0**-4
    return jnp.where(short, delta + error, rounded)


def encode_kernel(ids_hbm, owner_hbm, fresh_hbm, older_hbm, out_hbm, ids_ref, owner_ref, place_ref, fresh_ref, older_ref, value_ref, sems, few, sent):
    slots = fresh_ref.shape[0]
    ids = pltpu.make_async_copy(ids_hbm, ids_ref, few.at[0])
    owner = pltpu.make_async_copy(owner_hbm, owner_ref, few.at[1])
    ids.start()
    owner.start()
    copies = []
    for slot in range(slots):
        fresh = pltpu.make_async_copy(fresh_hbm.at[slot], fresh_ref.at[slot], sems.at[0, slot])
        older = pltpu.make_async_copy(older_hbm.at[slot], older_ref.at[slot], sems.at[1, slot])
        fresh.start()
        older.start()
        copies.append((fresh, older))
    for slot in range(slots):
        place_ref[slot] = -1
    ids.wait()
    owner.wait()
    for e in range(EXPERTS):
        place_ref[ids_ref[e]] = owner_ref[e]
    for slot, (fresh, older) in enumerate(copies):
        fresh.wait()
        older.wait()
        place = place_ref[slot]

        @pl.when(place >= 0)
        def _():
            value_ref[place] = quantize(fresh_ref[slot], older_ref[slot]).astype(jnp.bfloat16)
            pltpu.make_async_copy(value_ref.at[place], out_hbm.at[place], sent.at[place]).start()

    for e in range(EXPERTS):
        pltpu.make_async_copy(value_ref.at[e], out_hbm.at[e], sent.at[e]).wait()


def encode(updated, trainer_base, sync_ids, owner_map):
    slots = updated.shape[0]
    anywhere = pl.BlockSpec(memory_space=pl.ANY)
    return pl.pallas_call(
        encode_kernel,
        in_specs=[anywhere] * 4,
        out_specs=anywhere,
        out_shape=jax.ShapeDtypeStruct((EXPERTS, ROWS, BLOCK), jnp.bfloat16),
        scratch_shapes=[
            pltpu.SMEM((EXPERTS,), jnp.int32),
            pltpu.SMEM((EXPERTS,), jnp.int32),
            pltpu.SMEM((slots,), jnp.int32),
            pltpu.VMEM(updated.shape, jnp.bfloat16),
            pltpu.VMEM(updated.shape, jnp.bfloat16),
            pltpu.VMEM((EXPERTS, ROWS, BLOCK), jnp.bfloat16),
            pltpu.SemaphoreType.DMA((2, slots)),
            pltpu.SemaphoreType.DMA((2,)),
            pltpu.SemaphoreType.DMA((EXPERTS,)),
        ],
        name="encode",
    )(sync_ids, owner_map, updated, trainer_base)


def swaps(zh):
    return (zh + 1) // 2 % 2


def exchange(values):
    groups = []
    for y in range(4):
        for group in range(2):
            groups.append(
                [(y * 2 + (group ^ swaps(s // 8))) * 32 + s for s in range(32)]
            )
    return lax.all_to_all(
        values, ("rollout", "shard"), split_axis=0, concat_axis=0, axis_index_groups=groups, tiled=True
    )


def shifted(block, dy=0, dz=0):
    pairs = []
    for y in range(4):
        for z in range(2):
            pairs.append((y * 2 + z, (y + dy) % 4 * 2 + (z + dz) % 2))
    return lax.ppermute(block, "rollout", pairs)


def column_of(k, band):
    rollout, zh = lax.axis_index("rollout"), lax.axis_index("shard") // 8
    dy, dz = MOVES[k]
    y = (rollout // 2 + dy + 4) % 4
    z = (rollout + dz + swaps(zh) + swaps(band)) % 2
    return pl.ds(pl.multiple_of((y * 2 + z) * BLOCK, BLOCK), BLOCK)


def cut(spans, low, high):
    found = []
    for n, (start, stop) in enumerate(spans):
        a, b = max(start, low), min(stop, high)
        if a < b:
            found.append((n, pl.ds(a - start, b - a), a, b - a))
    return found


def add_kernel(spans, base_ref, *refs):
    parts, (out_ref, rest_ref) = refs[:-2], refs[-2:]
    band = pl.program_id(0)
    for k in range(FIRST, 8):
        rest_ref[k - FIRST] = base_ref[:, column_of(k, band)]
    for n in range(4):

        @pl.when(band == n)
        def _():
            first = 0
            for k in range(FIRST):
                columns = column_of(k, band)
                for which, rows, a, size in cut(spans[k], n * BAND, (n + 1) * BAND):
                    at = pl.ds(a - n * BAND, size)
                    out_ref[at, columns] = base_ref[at, columns] + parts[first + which][rows, :]
                first += len(spans[k])


def add(base, spans, parts):
    rows = pl.BlockSpec((BAND, WIDTH), lambda i: (i, 0))
    return pl.pallas_call(
        functools.partial(add_kernel, spans),
        grid=(OWNED // BAND,),
        in_specs=[rows] + [pl.BlockSpec(memory_space=pltpu.VMEM)] * len(parts),
        out_specs=[rows, pl.BlockSpec((8 - FIRST, BAND, BLOCK), lambda i: (0, i, 0))],
        out_shape=[
            jax.ShapeDtypeStruct((OWNED, WIDTH), jnp.bfloat16),
            jax.ShapeDtypeStruct((8 - FIRST, OWNED, BLOCK), jnp.bfloat16),
        ],
        compiler_params=pltpu.CompilerParams(vmem_limit_bytes=12 * 2**20),
        cost_estimate=pl.CostEstimate(flops=OWNED * WIDTH, bytes_accessed=6 * OWNED * WIDTH, transcendentals=0),
        name="add",
    )(base, *parts)


def finish_kernel(spans, rest_ref, *refs):
    parts, (out_hbm, total_ref, sems) = refs[:-4], refs[-3:]
    copies = []
    first = 0
    for n in range(8 - FIRST):
        for band in range(4):
            for which, rows, a, size in cut(spans[n], band * BAND, (band + 1) * BAND):
                total_ref[n, pl.ds(a, size), :] = rest_ref[n, pl.ds(a, size), :] + parts[first + which][rows, :]
            rows = pl.ds(band * BAND, BAND)
            to = out_hbm.at[rows, column_of(n + FIRST, band)]
            copies.append(pltpu.make_async_copy(total_ref.at[n, rows], to, sems.at[n, band]))
            copies[-1].start()
        first += len(spans[n])
    for copy in copies:
        copy.wait()


def finish(rest, spans, parts, made):
    whole = pl.BlockSpec(memory_space=pltpu.VMEM)
    return pl.pallas_call(
        functools.partial(finish_kernel, spans),
        in_specs=[whole] * (1 + len(parts)) + [pl.BlockSpec(memory_space=pl.ANY)],
        out_specs=pl.BlockSpec(memory_space=pl.ANY),
        out_shape=jax.ShapeDtypeStruct((OWNED, WIDTH), jnp.bfloat16),
        scratch_shapes=[pltpu.VMEM((8 - FIRST, OWNED, BLOCK), jnp.bfloat16), pltpu.SemaphoreType.DMA((8 - FIRST, 4))],
        input_output_aliases={1 + len(parts): 0},
        compiler_params=pltpu.CompilerParams(vmem_limit_bytes=8 * 2**20),
        name="finish",
    )(rest, *parts, made)


def join_kernel(a_ref, b_ref, below_ref, above_ref, whole_ref):
    whole_ref[:SPLIT] = a_ref[...]
    whole_ref[SPLIT:] = b_ref[...]


def joined(a, b, below, above):
    block = pl.BlockSpec(memory_space=pltpu.VMEM)
    anywhere = pl.BlockSpec(memory_space=pl.ANY)
    return pl.pallas_call(
        join_kernel,
        in_specs=[block, block, anywhere, anywhere],
        out_specs=block,
        out_shape=jax.ShapeDtypeStruct((OWNED, BLOCK), jnp.bfloat16),
        compiler_params=pltpu.CompilerParams(vmem_limit_bytes=2 * 2**20),
        name="joined",
    )(a, b, below, above)


def gather(own):
    own_a, own_b = own[:SPLIT], own[SPLIT:]
    below_a, above_b = shifted(own_a, dy=1), shifted(own_b, dy=-1)
    beside_a, beside_b = shifted(own_a, dz=1), shifted(own_b, dz=1)
    below_b, above_a = shifted(own_b, dy=1), shifted(own_a, dy=-1)
    far_a, far_b = shifted(below_a, dy=1), shifted(above_b, dy=-1)
    beside = joined(beside_a, beside_b, below_b, above_a)
    bb, ba = shifted(beside[:-EDGE], dy=1), shifted(beside[EDGE:], dy=-1)
    beside, first, last = lax.optimization_barrier((beside, above_a[:EDGE], below_b[-EDGE:]))
    edges = shifted(jnp.concatenate([first, last], axis=0), dz=1)
    top, bottom = edges[:EDGE], edges[EDGE:]
    fz_top, fz_bottom = shifted(top, dy=-1), shifted(bottom, dy=1)
    middle = shifted(jnp.concatenate([far_a[EDGE:], far_b[:-EDGE]], axis=0), dz=1)
    parts = [
        [(own_a, 0), (own_b, SPLIT)],
        [(above_a, 0), (above_b, SPLIT)],
        [(beside, 0)],
        [(below_a, 0), (below_b, SPLIT)],
        [(far_a, 0), (far_b, SPLIT)],
        [(top, 0), (ba, EDGE)],
        [(bb, 0), (bottom, OWNED - EDGE)],
        [(fz_top, 0), (middle, EDGE), (fz_bottom, OWNED - EDGE)],
    ]
    spans = [[(start, start + piece.shape[0]) for piece, start in pieces] for pieces in parts]
    return [[piece for piece, _ in pieces] for pieces in parts], spans


def per_device(updated, trainer_base, rollout_base, sync_ids, owner_map):
    values = encode(updated, trainer_base, sync_ids, owner_map).reshape(32, PIECE, BLOCK)
    parts, spans = gather(exchange(values).reshape(OWNED, BLOCK))
    flat = lambda some: [piece for pieces in some for piece in pieces]
    made, rest = add(rollout_base[0], spans[:FIRST], flat(parts[:FIRST]))
    return finish(rest, spans[FIRST:], flat(parts[FIRST:]), made)[None]


def solution(mesh):
    return jax.shard_map(
        per_device,
        mesh=mesh,
        in_specs=(
            P(None, "shard", "rollout"),
            P(None, "shard", "rollout"),
            P("shard", None, None),
            P(),
            P(),
        ),
        out_specs=P("shard", None, None),
        check_vma=False,
    )
```

```python
import functools

import jax
import jax.numpy as jnp
from jax import lax
from jax.experimental import pallas as pl
from jax.experimental.pallas import tpu as pltpu
from jax.sharding import PartitionSpec as P

EXPERTS = 8
ROWS = 224
BLOCK = 128
PIECE = 56
OWNED = 1792
WIDTH = 1024
BAND = 448
SPLIT = 896
FIRST = 5
MOVES = [(0, 0), (1, 0), (0, 1), (-1, 0), (2, 0), (1, 1), (-1, 1), (2, 1)]


def leading(magnitude):
    spread = magnitude * (2.0**23 + 1.0)
    return spread - (spread - magnitude)


def quantize(fresh, older):
    delta = fresh.astype(jnp.float32) - older.astype(jnp.float32)
    magnitude = jnp.abs(delta)
    largest = jnp.max(magnitude, axis=-1, keepdims=True)
    power = leading(largest)
    least = jnp.where(largest > 0.875 * power, power * 2.0**-14, power * 2.0**-15)
    least = jnp.maximum(least, 2.0**-30)
    power = leading(magnitude)
    binade = jnp.maximum(jnp.where(power > magnitude, power * 0.5, power), least)
    shift = binade * (1.5 * 2.0**20)
    rounded = (delta + shift) - shift
    error = delta - rounded
    short = (magnitude - jnp.abs(rounded)) >= binade * 2.0**-4
    return jnp.where(short, delta + error, rounded)


def encode_kernel(ids_hbm, owner_hbm, fresh_hbm, older_hbm, out_hbm, ids_ref, owner_ref, place_ref, fresh_ref, older_ref, value_ref, sems, few, sent):
    slots = fresh_ref.shape[0]
    ids = pltpu.make_async_copy(ids_hbm, ids_ref, few.at[0])
    owner = pltpu.make_async_copy(owner_hbm, owner_ref, few.at[1])
    ids.start()
    owner.start()
    copies = []
    for slot in range(slots):
        fresh = pltpu.make_async_copy(fresh_hbm.at[slot], fresh_ref.at[slot], sems.at[0, slot])
        older = pltpu.make_async_copy(older_hbm.at[slot], older_ref.at[slot], sems.at[1, slot])
        fresh.start()
        older.start()
        copies.append((fresh, older))
    for slot in range(slots):
        place_ref[slot] = -1
    ids.wait()
    owner.wait()
    for e in range(EXPERTS):
        place_ref[ids_ref[e]] = owner_ref[e]
    for slot, (fresh, older) in enumerate(copies):
        fresh.wait()
        older.wait()
        place = place_ref[slot]

        @pl.when(place >= 0)
        def _():
            value_ref[place] = quantize(fresh_ref[slot], older_ref[slot]).astype(jnp.bfloat16)
            pltpu.make_async_copy(value_ref.at[place], out_hbm.at[place], sent.at[place]).start()

    for e in range(EXPERTS):
        pltpu.make_async_copy(value_ref.at[e], out_hbm.at[e], sent.at[e]).wait()


def encode(updated, trainer_base, sync_ids, owner_map):
    slots = updated.shape[0]
    anywhere = pl.BlockSpec(memory_space=pl.ANY)
    return pl.pallas_call(
        encode_kernel,
        in_specs=[anywhere] * 4,
        out_specs=anywhere,
        out_shape=jax.ShapeDtypeStruct((EXPERTS, ROWS, BLOCK), jnp.bfloat16),
        scratch_shapes=[
            pltpu.SMEM((EXPERTS,), jnp.int32),
            pltpu.SMEM((EXPERTS,), jnp.int32),
            pltpu.SMEM((slots,), jnp.int32),
            pltpu.VMEM(updated.shape, jnp.bfloat16),
            pltpu.VMEM(updated.shape, jnp.bfloat16),
            pltpu.VMEM((EXPERTS, ROWS, BLOCK), jnp.bfloat16),
            pltpu.SemaphoreType.DMA((2, slots)),
            pltpu.SemaphoreType.DMA((2,)),
            pltpu.SemaphoreType.DMA((EXPERTS,)),
        ],
        name="encode",
    )(sync_ids, owner_map, updated, trainer_base)


def swaps(zh):
    return zh // 2 % 2


def exchange(values):
    groups = []
    for y in range(4):
        for group in range(2):
            groups.append(
                [(y * 2 + (group ^ swaps(s // 8))) * 32 + s for s in range(32)]
            )
    return lax.all_to_all(
        values, ("rollout", "shard"), split_axis=0, concat_axis=0, axis_index_groups=groups, tiled=True
    )


def shifted(block, dy=0, dz=0):
    pairs = []
    for y in range(4):
        for z in range(2):
            pairs.append((y * 2 + z, (y + dy) % 4 * 2 + (z + dz) % 2))
    return lax.ppermute(block, "rollout", pairs)


def column_of(k, band):
    rollout, zh = lax.axis_index("rollout"), lax.axis_index("shard") // 8
    dy, dz = MOVES[k]
    y = (rollout // 2 + dy + 4) % 4
    z = (rollout + dz + swaps(zh) + swaps(band)) % 2
    return pl.ds(pl.multiple_of((y * 2 + z) * BLOCK, BLOCK), BLOCK)


def cut(spans, low, high):
    found = []
    for n, (start, stop) in enumerate(spans):
        a, b = max(start, low), min(stop, high)
        if a < b:
            found.append((n, pl.ds(a - start, b - a), a, b - a))
    return found


def add_kernel(spans, base_ref, *refs):
    parts, (out_ref, rest_ref) = refs[:-2], refs[-2:]
    band = pl.program_id(0)
    for k in range(FIRST, 8):
        rest_ref[k - FIRST] = base_ref[:, column_of(k, band)]
    for n in range(4):

        @pl.when(band == n)
        def _():
            first = 0
            for k in range(FIRST):
                columns = column_of(k, band)
                for which, rows, a, size in cut(spans[k], n * BAND, (n + 1) * BAND):
                    at = pl.ds(a - n * BAND, size)
                    out_ref[at, columns] = base_ref[at, columns] + parts[first + which][rows, :]
                first += len(spans[k])


def add(base, spans, parts):
    rows = pl.BlockSpec((BAND, WIDTH), lambda i: (i, 0))
    return pl.pallas_call(
        functools.partial(add_kernel, spans),
        grid=(OWNED // BAND,),
        in_specs=[rows] + [pl.BlockSpec(memory_space=pltpu.VMEM)] * len(parts),
        out_specs=[rows, pl.BlockSpec((8 - FIRST, BAND, BLOCK), lambda i: (0, i, 0))],
        out_shape=[
            jax.ShapeDtypeStruct((OWNED, WIDTH), jnp.bfloat16),
            jax.ShapeDtypeStruct((8 - FIRST, OWNED, BLOCK), jnp.bfloat16),
        ],
        compiler_params=pltpu.CompilerParams(vmem_limit_bytes=12 * 2**20),
        cost_estimate=pl.CostEstimate(flops=OWNED * WIDTH, bytes_accessed=6 * OWNED * WIDTH, transcendentals=0),
        name="add",
    )(base, *parts)


def finish_kernel(spans, rest_ref, *refs):
    parts, (out_hbm, total_ref, sems) = refs[:-4], refs[-3:]
    copies = []
    first = 0
    for n in range(8 - FIRST):
        for band in range(4):
            for which, rows, a, size in cut(spans[n], band * BAND, (band + 1) * BAND):
                total_ref[n, pl.ds(a, size), :] = rest_ref[n, pl.ds(a, size), :] + parts[first + which][rows, :]
            rows = pl.ds(band * BAND, BAND)
            to = out_hbm.at[rows, column_of(n + FIRST, band)]
            copies.append(pltpu.make_async_copy(total_ref.at[n, rows], to, sems.at[n, band]))
            copies[-1].start()
        first += len(spans[n])
    for copy in copies:
        copy.wait()


def finish(rest, spans, parts, made):
    whole = pl.BlockSpec(memory_space=pltpu.VMEM)
    return pl.pallas_call(
        functools.partial(finish_kernel, spans),
        in_specs=[whole] * (1 + len(parts)) + [pl.BlockSpec(memory_space=pl.ANY)],
        out_specs=pl.BlockSpec(memory_space=pl.ANY),
        out_shape=jax.ShapeDtypeStruct((OWNED, WIDTH), jnp.bfloat16),
        scratch_shapes=[pltpu.VMEM((8 - FIRST, OWNED, BLOCK), jnp.bfloat16), pltpu.SemaphoreType.DMA((8 - FIRST, 4))],
        input_output_aliases={1 + len(parts): 0},
        compiler_params=pltpu.CompilerParams(vmem_limit_bytes=8 * 2**20),
        name="finish",
    )(rest, *parts, made)


def join_kernel(a_ref, b_ref, below_ref, above_ref, whole_ref):
    whole_ref[:SPLIT] = a_ref[...]
    whole_ref[SPLIT:] = b_ref[...]


def joined(a, b, below, above):
    block = pl.BlockSpec(memory_space=pltpu.VMEM)
    anywhere = pl.BlockSpec(memory_space=pl.ANY)
    return pl.pallas_call(
        join_kernel,
        in_specs=[block, block, anywhere, anywhere],
        out_specs=block,
        out_shape=jax.ShapeDtypeStruct((OWNED, BLOCK), jnp.bfloat16),
        compiler_params=pltpu.CompilerParams(vmem_limit_bytes=2 * 2**20),
        name="joined",
    )(a, b, below, above)


def gather(own):
    own_a, own_b = own[:SPLIT], own[SPLIT:]
    below_a, above_b = shifted(own_a, dy=1), shifted(own_b, dy=-1)
    beside_a, beside_b = shifted(own_a, dz=1), shifted(own_b, dz=1)
    below_b, above_a = shifted(own_b, dy=1), shifted(own_a, dy=-1)
    far_a, far_b = shifted(below_a, dy=1), shifted(above_b, dy=-1)
    beside = joined(beside_a, beside_b, below_b, above_a)
    bb, ba = shifted(beside, dy=1), shifted(beside, dy=-1)
    fz_a, fz_b = shifted(far_a, dz=1), shifted(far_b, dz=1)
    parts = [
        [(own_a, 0), (own_b, SPLIT)],
        [(above_a, 0), (above_b, SPLIT)],
        [(beside, 0)],
        [(below_a, 0), (below_b, SPLIT)],
        [(far_a, 0), (far_b, SPLIT)],
        [(ba, 0)],
        [(bb, 0)],
        [(fz_a, 0), (fz_b, SPLIT)],
    ]
    spans = [[(start, start + piece.shape[0]) for piece, start in pieces] for pieces in parts]
    return [[piece for piece, _ in pieces] for pieces in parts], spans


def per_device(updated, trainer_base, rollout_base, sync_ids, owner_map):
    values = encode(updated, trainer_base, sync_ids, owner_map).reshape(32, PIECE, BLOCK)
    parts, spans = gather(exchange(values).reshape(OWNED, BLOCK))
    flat = lambda some: [piece for pieces in some for piece in pieces]
    made, rest = add(rollout_base[0], spans[:FIRST], flat(parts[:FIRST]))
    return finish(rest, spans[FIRST:], flat(parts[FIRST:]), made)[None]


def solution(mesh):
    return jax.shard_map(
        per_device,
        mesh=mesh,
        in_specs=(
            P(None, "shard", "rollout"),
            P(None, "shard", "rollout"),
            P("shard", None, None),
            P(),
            P(),
        ),
        out_specs=P("shard", None, None),
        check_vma=False,
    )
```
